32 devices in a mesh: tile: 8 (over z, y), slab: 4 (over x, core).
Axes of the slice: x: 2, y: 2, z: 4, core: 2. Of those that a mesh axis runs over, the one named last changes fastest.
Arguments:
- volume: bfloat16 [8, 64, 64, 256], P('tile', 'slab'), may hold values from -24 to 24
- partner: int32 [8], replicated, may hold values from 0 to 7, as said below
- offsets: int32 [8], replicated, may hold values from 0 to 7
- starts: int32 [512], P(('tile', 'slab')), may hold values from 0 to 192
- classifier: int32 [512, 1], P(('tile', 'slab')), may hold values from 0 to 7; in each aligned block of 16 rows (0 to 15, 16 to 31, ...) at most 2 rows name the same one
- stem_weight: bfloat16 [8, 512, 256], P('tile'), may hold values from -0.25 to 0.25
- expand_weight: bfloat16 [8, 1, 256, 1024], P('tile'), may hold values from -0.375 to 0.375
- shrink_weight: bfloat16 [8, 1, 1024, 256], P('tile'), may hold values from -0.1875 to 0.1875
- head_weight: bfloat16 [8, 256, 8], P('tile'), may hold values from -0.375 to 0.375
Outputs:
- log_response: float32 [8, 64, 64, 256], P('tile', 'slab')
- logits: float32 [512, 8], P(('tile', 'slab'))
The draws below stay inside these ranges and needn't reach their ends.
Inputs may be any that keep to these rules, and one draw needn't show every extreme that they name: partner[partner[t]] = t and partner[t] != t for every tile t. Among the 16 candidates of one device at most 2 name the same classifier.
All inputs are finite; a program needn't handle non-finite values.
Results may differ from the reference program's by a relative error of at most 0.0024.
Values may be sent and summed in bfloat16 or wider, within the bound.
A program may use at most 320 MiB of HBM per device.

```python
import math
import jax
import jax.numpy as jnp
import numpy as np
from jax import lax

ZD = 16
YW = 64
XW = 256
OV = 32
OFFMAX = 8
CX = 64
CAND_DEV = 16
CAP = 2
C = 256
HID = 1024
NCLS = 8
BLOCKS = 1
PATCH = 512
TILES = 8
NZ = 64
CANDS = 512
CLASSIFIERS = 8
N_TILE = 8
N_SLAB = 4


def draw_partner(key, part):
    half = TILES // 2
    first_key = jax.random.fold_in(key, 11)
    order_key = jax.random.fold_in(key, 12)
    anchor = jax.random.randint(first_key, (), 0, half).astype(jnp.int32)
    mate = anchor + half
    tile_ids = jnp.arange(TILES, dtype=jnp.int32)
    ranks = jax.random.permutation(order_key, tile_ids)
    ranks = jnp.where(tile_ids == anchor, -2, ranks)
    ranks = jnp.where(tile_ids == mate, -1, ranks)
    order = jnp.argsort(ranks, stable=True).astype(jnp.int32)
    paired = order.reshape(half, 2)
    matched = jnp.zeros((TILES,), jnp.int32)
    matched = matched.at[paired[:, 0]].set(paired[:, 1])
    matched = matched.at[paired[:, 1]].set(paired[:, 0])
    return matched


def with_ends(values, key, smallest, high):
    shape = values.shape
    spot = [jax.random.randint(jax.random.fold_in(key, axis), (), 0, shape[axis]) for axis in range(len(shape))]
    values = values.at[tuple(spot)].set(smallest)
    longest = shape.index(max(shape))
    spot[longest] = (spot[longest] + 1) % shape[longest]
    return values.at[tuple(spot)].set(high)


def block_scale(own_key, shape, pieces, smallest, top_value):
    factor_of, own = 1.0, jax.random.fold_in(own_key, 6)
    for position, blocks in pieces:
        heights = jnp.exp(jax.random.uniform(jax.random.fold_in(own, position), (blocks,), jnp.float32, smallest / len(pieces), top_value / len(pieces)))
        factor_of = factor_of * jnp.repeat(heights, shape[position] // blocks).reshape([-1 if axis == position else 1 for axis in range(len(shape))])
    return factor_of


def shared_out(key, own, number, rows, count, top, reach, lean):
    ranking = jax.random.permutation(key, count)
    packed, ordinary = load_shares(count, rows * top, reach, lean, True), load_shares(count, rows * top, reach, lean, False)
    places = jnp.arange(count)

    def named(sizes, turn):
        used = int((sizes > 0).sum())
        fixed = max(1, used // 4)
        shifted = fixed + (places - fixed + turn * (used - fixed)) % max(1, count - fixed)
        return jnp.zeros((count,), jnp.int32).at[ranking[jnp.where(places < fixed, places, shifted)]].set(jnp.asarray(sizes, jnp.int32))

    sizes = jnp.where(number % 4 == 0, named(packed, number // 4), named(ordinary, number - number // 4 - 1))
    mixed = jax.random.permutation(jax.random.fold_in(own, 3), count)
    source_of, sink = mixed[0:count // 2 * 2:2], mixed[1:count // 2 * 2:2]
    slack = jnp.minimum(sizes[source_of] - 1, reach - sizes[sink]) // 2
    slack = jnp.where((source_of == ranking[0]) | (sink == ranking[0]) | (sizes[sink] == 0), 0, jnp.maximum(slack, 0))
    shifted = jax.random.randint(jax.random.fold_in(own, 4), (count // 2,), 0, 1 << 20) % (slack + 1)
    sizes = sizes.at[source_of].add(-shifted).at[sink].add(shifted)
    labels = jnp.searchsorted(jnp.cumsum(sizes), jnp.arange(rows * top), side="right").astype(jnp.int32)
    grid = labels.reshape(top, rows).T
    grid = grid[jax.random.permutation(jax.random.fold_in(own, 1), rows)]
    turn = jax.random.randint(jax.random.fold_in(own, 2), (rows, 1), 0, top)
    return jnp.take_along_axis(grid, (jnp.arange(top)[None, :] + turn) % top, axis=1)


def load_shares(amount, total, reach, lean, full):
    loads = [(1 << 20) // math.isqrt(rank ** lean) + 1 for rank in range(1, amount + 1)]
    largest = reach if full else min(reach, max(-(-total // amount), total * loads[0] // sum(loads)))
    least = 1 if total - largest >= amount - 1 else 0
    counts, surplus = [largest] + [least] * (amount - 1), total - largest - least * (amount - 1)
    while surplus > 0:
        free = [i for i in range(1, amount) if counts[i] < largest] or [i for i in range(1, amount) if counts[i] < reach]
        mass, remaining = sum([loads[i] for i in free]), surplus
        for i in free:
            addition = min(reach - counts[i], max(1, remaining * loads[i] // mass), surplus)
            counts[i] = counts[i] + addition
            surplus = surplus - addition
    return np.array(counts)


def normal_values(rng, shape, spread, most, split=(), kind=jnp.bfloat16):
    result = jax.random.normal(rng, shape, jnp.float32) * spread
    if len(split) > 0:
        result = block_scale(rng, shape, split, -0.22, 0.18) * result
    return jnp.clip(result, min=-most, max=most).astype(kind)


def setup_inputs(seed: int = 0) -> dict:
    key_list = jax.random.split(jax.random.key(seed), 10)
    volume = normal_values(key_list[0], (TILES, NZ, YW, XW), 4.0, 24.0, ((0, 8), (1, 4)))
    partner = draw_partner(jax.random.fold_in(key_list[9], 71), 0)
    offsets = with_ends(jax.random.randint(key_list[2], (TILES,), 0, OFFMAX), jax.random.fold_in(key_list[2], 1), 0, OFFMAX - 1).astype(jnp.int32)
    starts = with_ends(jax.random.randint(key_list[3], (CANDS,), 0, XW - CX + 1), jax.random.fold_in(key_list[3], 1), 0, XW - CX).astype(jnp.int32)
    classifier_keys = jax.random.split(jax.random.fold_in(key_list[4], 1), CANDS // CAND_DEV)
    classifier_turns = jax.random.permutation(jax.random.fold_in(key_list[4], 3), CANDS // CAND_DEV)
    classifier = jax.vmap(lambda own, number: shared_out(jax.random.fold_in(key_list[4], 2), own, number, CAND_DEV, CLASSIFIERS, 1, CAP, 2))(classifier_keys, classifier_turns).reshape((CANDS, 1))
    stem_weight = normal_values(key_list[5], (CLASSIFIERS, PATCH, C), PATCH ** -0.5, 0.25, ((0, 8),))
    expand_weight = normal_values(key_list[6], (CLASSIFIERS, BLOCKS, C, HID), C ** -0.5, 0.375, ((0, 8),))
    shrink_weight = normal_values(key_list[7], (CLASSIFIERS, BLOCKS, HID, C), HID ** -0.5, 0.1875, ((0, 8),))
    head_weight = normal_values(key_list[8], (CLASSIFIERS, C, NCLS), C ** -0.5, 0.375, ((0, 8),))
    return dict(volume=volume, partner=partner, offsets=offsets, starts=starts, classifier=classifier, stem_weight=stem_weight, expand_weight=expand_weight, shrink_weight=shrink_weight, head_weight=head_weight)


RADIUS = 3

def gauss_taps():
    weights_raw = [math.exp(-0.5 * j * j) for j in range(-RADIUS, RADIUS + 1)]
    summed = sum(weights_raw)
    return [value / summed for value in weights_raw]

def taps_sum(padded, axis, length):
    coeffs = gauss_taps()
    running = coeffs[0] * lax.slice_in_dim(padded, 0, length, axis=axis)
    for offset_tap in range(1, 2 * RADIUS + 1):
        running = running + coeffs[offset_tap] * lax.slice_in_dim(padded, offset_tap, offset_tap + length, axis=axis)
    return running

def smooth_axis(values, axis):
    padding = [(0, 0)] * values.ndim
    padding[axis] = (RADIUS, RADIUS)
    return taps_sum(jnp.pad(values, padding), axis, values.shape[axis])

def laplace(values):
    padded = jnp.pad(values, ((0, 0), (1, 1), (1, 1), (1, 1)))
    beside = padded[:, 2:, 1:-1, 1:-1] + padded[:, :-2, 1:-1, 1:-1]
    beside = beside + padded[:, 1:-1, 2:, 1:-1] + padded[:, 1:-1, :-2, 1:-1]
    beside = beside + padded[:, 1:-1, 1:-1, 2:] + padded[:, 1:-1, 1:-1, :-2]
    return beside - 6.0 * values

def patchify(cube_block):
    chans, planes, height, across = cube_block.shape
    shaped = cube_block.reshape(chans, planes // 4, 4, height // 8, 8, across // 8, 8)
    shaped = shaped.transpose(1, 3, 5, 0, 2, 4, 6)
    return shaped.reshape(planes // 4 * (height // 8) * (across // 8), chans * 256)

def classify(patches, stems, expands, shrinks, heads):
    hidden = jnp.einsum('npf,nfk->npk', patches.astype(jnp.float32), stems.astype(jnp.float32)).astype(jnp.bfloat16)
    for block_id in range(BLOCKS):
        wide = hidden.astype(jnp.float32)
        normed = (wide * lax.rsqrt(lax.optimization_barrier(jnp.mean(wide * wide, axis=-1, keepdims=True)) + 1e-05)).astype(jnp.bfloat16)
        expanded = jax.nn.relu(jnp.einsum('npk,nkh->nph', normed.astype(jnp.float32), expands[:, block_id].astype(jnp.float32))).astype(jnp.bfloat16)
        hidden = (wide + jnp.einsum('nph,nhk->npk', expanded.astype(jnp.float32), shrinks[:, block_id].astype(jnp.float32))).astype(jnp.bfloat16)
    pooled = lax.optimization_barrier(jnp.mean(hidden.astype(jnp.float32), axis=1))
    return jnp.einsum('nk,nkc->nc', pooled, heads.astype(jnp.float32), precision=lax.Precision.HIGHEST)

def reference(volume, partner, offsets, starts, classifier, stem_weight, expand_weight, shrink_weight, head_weight):
    values = volume.astype(jnp.float32)
    mates = volume[partner][..., :OV].astype(jnp.float32)
    row_ids = (jnp.arange(YW, dtype=jnp.int32)[None, :] - offsets[:, None]) % YW
    mates = jnp.take_along_axis(mates, row_ids[:, None, :, None], axis=2)
    column = jnp.arange(OV, dtype=jnp.float32)
    ramp = 0.25 + 0.5 * (column + 0.5) / OV
    blended = ramp * values[..., :OV] + (1.0 - ramp) * mates
    joined = jnp.concatenate([blended, values[..., OV:]], axis=3)
    smooth = smooth_axis(smooth_axis(smooth_axis(joined, 1), 2), 3)
    log_response = laplace(smooth)
    channel_pair = jnp.stack([smooth.astype(jnp.bfloat16), log_response.astype(jnp.bfloat16)], axis=1)
    zero = jnp.zeros((), jnp.int32)

    def one_device(device):
        tile_id = (device // N_SLAB).astype(jnp.int32)
        slab_id = (device % N_SLAB).astype(jnp.int32)
        band = lax.dynamic_slice(channel_pair, (tile_id, zero, slab_id * ZD, zero, zero), (1, 2, ZD, YW, XW))[0]
        first = (device * CAND_DEV).astype(jnp.int32)
        own_starts = lax.dynamic_slice_in_dim(starts, first, CAND_DEV)
        own_routes = lax.dynamic_slice_in_dim(classifier[:, 0], first, CAND_DEV)

        def cut(begin):
            return patchify(lax.dynamic_slice(band, (zero, zero, zero, begin.astype(jnp.int32)), (2, ZD, YW, CX)))
        patches = jax.vmap(cut)(own_starts)
        return classify(patches, stem_weight[own_routes], expand_weight[own_routes], shrink_weight[own_routes], head_weight[own_routes])
    scores = lax.map(one_device, jnp.arange(N_TILE * N_SLAB, dtype=jnp.int32))
    return (log_response, scores.reshape(CANDS, NCLS))
```

```python
import functools
import math

import jax
import jax.numpy as jnp
from jax import lax
from jax.experimental import pallas as pl
from jax.experimental.pallas import tpu as pltpu
from jax.sharding import PartitionSpec as P

OV = 32
RADIUS = 3
HALO = RADIUS + 1
PAD = 8


def gauss_taps():
    weights_raw = [math.exp(-0.5 * j * j) for j in range(-RADIUS, RADIUS + 1)]
    summed = sum(weights_raw)
    return [value / summed for value in weights_raw]


def band_kernel(flags_ref, joined_ref, band_ref, log_ref, table_ref, smooth, lateral, turned):
    planes, rows, width = log_ref.shape
    taps = gauss_taps()
    zero_rows = jnp.zeros((PAD, width), jnp.float32)

    lateral[0:PAD] = zero_rows
    lateral[PAD + rows :] = zero_rows

    @pl.loop(0, planes + 2)
    def _(z):
        total = taps[RADIUS] * joined_ref[z + RADIUS]
        for j in range(RADIUS):
            total = total + taps[j] * (joined_ref[z + j] + joined_ref[z + 2 * RADIUS - j])
        lateral[PAD : PAD + rows] = total
        down = taps[RADIUS] * total
        for j in range(RADIUS):
            shift = RADIUS - j
            down = down + taps[j] * (
                lateral[PAD - shift : PAD - shift + rows] + lateral[PAD + shift : PAD + shift + rows]
            )
        across = jnp.dot(
            down, band_ref[...], precision=lax.Precision.HIGHEST, preferred_element_type=jnp.float32
        )
        keep = jnp.where(z == 0, flags_ref[0], jnp.where(z == planes + 1, flags_ref[1], 1.0))
        smooth[z, 0:PAD] = zero_rows
        smooth[z, PAD + rows :] = zero_rows
        smooth[z, PAD : PAD + rows] = across * keep

    column = lax.broadcasted_iota(jnp.int32, (rows, width), 1)

    @pl.loop(0, planes)
    def _(z):
        center = smooth[z + 1, PAD : PAD + rows]
        beside = smooth[z, PAD : PAD + rows] + smooth[z + 2, PAD : PAD + rows]
        beside = beside + smooth[z + 1, PAD + 1 : PAD + 1 + rows] + smooth[z + 1, PAD - 1 : PAD - 1 + rows]
        right = jnp.where(column == width - 1, 0.0, pltpu.roll(center, width - 1, 1))
        left = jnp.where(column == 0, 0.0, pltpu.roll(center, 1, 1))
        log_ref[z] = beside + right + left - 6.0 * center

    pitch = turned.shape[0] // (planes // 4 * (rows // 8))

    @pl.loop(0, planes // 4)
    def _(a):
        for b in range(rows // 8):
            parts = [smooth[4 * a + dz + 1, PAD + 8 * b : PAD + 8 * b + 8] for dz in range(4)]
            parts = parts + [log_ref[4 * a + dz, 8 * b : 8 * b + 8] for dz in range(4)]
            block = jnp.concatenate(parts, axis=0)
            block = jnp.concatenate([block, pltpu.roll(block, width - 1, 1)], axis=0)
            start = pl.multiple_of((a * (rows // 8) + b) * pitch, 8)
            turned[pl.ds(start, width)] = block.T

    spots = planes // 4 * (rows // 8)

    @pl.loop(0, width // 8)
    def _(xb):
        for u in range(8):
            x = xb * 8 + u
            table_ref[x] = turned[pl.ds(x, spots, stride=pitch), :].astype(jnp.bfloat16)


def classify_kernel(starts_ref, routes_ref, table_ref, weights_ref, out_ref):
    slabs = weights_ref.shape[1]
    stem_rows, expand_rows, shrink_rows = 512 // slabs, 256 // slabs, 1024 // slabs

    def rows_of(route, first, length):
        return jnp.concatenate([weights_ref[route, s, first : first + length] for s in range(slabs)], axis=0)

    @pl.loop(0, out_ref.shape[0])
    def _(i):
        start = starts_ref[i]
        route = routes_ref[i]
        patches = jnp.concatenate(
            [
                jnp.concatenate([table_ref[start + 8 * c + 2 * j] for j in range(4)], axis=1)
                for c in range(8)
            ],
            axis=0,
        )
        stem = rows_of(route, 0, stem_rows)
        hidden = jnp.dot(patches, stem, preferred_element_type=jnp.float32).astype(jnp.bfloat16)
        wide = hidden.astype(jnp.float32)
        scale = lax.rsqrt(jnp.mean(wide * wide, axis=1, keepdims=True) + 1e-05)
        normed = (wide * scale).astype(jnp.bfloat16)
        expanded = []
        for block in range(4):
            expand = rows_of(route, stem_rows + block * expand_rows, expand_rows)
            wider = jnp.dot(normed, expand, preferred_element_type=jnp.float32)
            expanded.append(jnp.maximum(wider, 0.0).astype(jnp.bfloat16))
        shrink = rows_of(route, stem_rows + 4 * expand_rows, shrink_rows)
        added = jnp.dot(jnp.concatenate(expanded, axis=1), shrink, preferred_element_type=jnp.float32)
        last = (wide + added).astype(jnp.bfloat16).astype(jnp.float32)
        head = weights_ref[route, 0, stem_rows + 4 * expand_rows + shrink_rows :].astype(jnp.float32)
        total = head[0:8] * jnp.sum(last, axis=0, keepdims=True)
        score = jnp.sum(total, axis=1, keepdims=True) * (1.0 / patches.shape[0])
        out_ref[i] = jnp.broadcast_to(score, out_ref.shape[1:])


def own_weights(stem_weight, expand_weight, shrink_weight, head_weight):
    slabs, slab_me = lax.axis_size("slab"), lax.axis_index("slab")
    stem, expand, shrink, head = stem_weight[0], expand_weight[0, 0], shrink_weight[0, 0], head_weight[0]
    stem = lax.dynamic_slice_in_dim(stem.reshape(64, 8, 256), slab_me * (8 // slabs), 8 // slabs, axis=1)
    stem = stem.transpose(1, 0, 2).reshape(512 // slabs, 256)
    expand = lax.dynamic_slice_in_dim(expand, slab_me * (256 // slabs), 256 // slabs, axis=0)
    expand = [expand[:, 256 * m : 256 * m + 256] for m in range(4)]
    shrink = lax.dynamic_slice_in_dim(shrink, slab_me * (1024 // slabs), 1024 // slabs, axis=0)
    head = jnp.pad(head.T, ((0, 8), (0, 0)))
    return jnp.concatenate([stem] + expand + [shrink, head], axis=0)


def body(
    volume,
    partner,
    offsets,
    starts,
    classifier,
    stem_weight,
    expand_weight,
    shrink_weight,
    head_weight,
):
    slabs, slab_me = lax.axis_size("slab"), lax.axis_index("slab")
    tiles, tile_me = lax.axis_size("tile"), lax.axis_index("tile")
    planes, rows, width = volume.shape[1:]
    raw = volume[0]

    up = [(i, i + 1) for i in range(slabs - 1)]
    down = [(i + 1, i) for i in range(slabs - 1)]
    before = lax.ppermute(raw[planes - HALO :], "slab", up)
    after = lax.ppermute(raw[:HALO], "slab", down)
    raw = jnp.concatenate([before, raw, after], axis=0)
    deep = planes + 2 * HALO
    strips = lax.all_gather(raw[:, :, :OV], "tile", axis=0)

    share = own_weights(stem_weight, expand_weight, shrink_weight, head_weight)
    weights = lax.all_gather(share, ("tile", "slab"), axis=0)
    weights = weights.reshape(tiles, slabs, share.shape[0], 256)

    mate = lax.dynamic_index_in_dim(strips, partner[tile_me], 0, keepdims=False)
    mate = lax.dynamic_slice_in_dim(
        jnp.concatenate([mate, mate], axis=1), rows - offsets[tile_me], rows, axis=1
    ).astype(jnp.float32)
    ramp = 0.25 + 0.5 * (jnp.arange(OV, dtype=jnp.float32) + 0.5) / OV
    values = raw.astype(jnp.float32)
    joined = jnp.concatenate(
        [ramp * values[..., :OV] + (1.0 - ramp) * mate, values[..., OV:]], axis=2
    )

    taps = gauss_taps()
    apart = jnp.arange(width)[:, None] - jnp.arange(width)[None, :]
    band = sum(jnp.where(apart == j - RADIUS, taps[j], 0.0) for j in range(2 * RADIUS + 1))
    flags = jnp.stack([slab_me > 0, slab_me < slabs - 1]).astype(jnp.float32)
    spots = planes // 4 * (rows // 8)
    vmem = pl.BlockSpec(memory_space=pltpu.VMEM)
    smem = pl.BlockSpec(memory_space=pltpu.SMEM)
    log_response, table = pl.pallas_call(
        band_kernel,
        out_shape=(
            jax.ShapeDtypeStruct((planes, rows, width), jnp.float32),
            jax.ShapeDtypeStruct((width, spots, 128), jnp.bfloat16),
        ),
        in_specs=[smem, vmem, vmem],
        out_specs=(vmem, vmem),
        scratch_shapes=[
            pltpu.VMEM((planes + 2, rows + 2 * PAD, width), jnp.float32),
            pltpu.VMEM((rows + 2 * PAD, width), jnp.float32),
            pltpu.VMEM((spots * (width + 8), 128), jnp.float32),
        ],
        compiler_params=pltpu.CompilerParams(vmem_limit_bytes=48 * 1024 * 1024),
        cost_estimate=pl.CostEstimate(flops=10**9, bytes_accessed=6 * 10**6, transcendentals=0),
        name="band",
    )(flags, joined, band)

    count = starts.shape[0]
    scores = pl.pallas_call(
        classify_kernel,
        out_shape=jax.ShapeDtypeStruct((count, 8, 128), jnp.float32),
        in_specs=[smem, smem, vmem, vmem],
        out_specs=vmem,
        compiler_params=pltpu.CompilerParams(vmem_limit_bytes=48 * 1024 * 1024),
        cost_estimate=pl.CostEstimate(flops=54 * 10**8, bytes_accessed=13 * 10**6, transcendentals=0),
        name="classify",
    )(starts, classifier[:, 0], table, weights)
    return log_response[None], scores[:, :, 0]


def solution(mesh):
    return jax.shard_map(
        body,
        mesh=mesh,
        in_specs=(
            P("tile", "slab", None, None),
            P(),
            P(),
            P(("tile", "slab")),
            P(("tile", "slab"), None),
            P("tile", None, None),
            P("tile", None, None, None),
            P("tile", None, None, None),
            P("tile", None, None),
        ),
        out_specs=(P("tile", "slab", None, None), P(("tile", "slab"), None)),
        check_vma=False,
    )
```

```python
import functools
import math

import jax
import jax.numpy as jnp
from jax import lax
from jax.experimental import pallas as pl
from jax.experimental.pallas import tpu as pltpu
from jax.sharding import PartitionSpec as P

OV = 32
RADIUS = 3
HALO = RADIUS + 1
PAD = 8


def gauss_taps():
    weights_raw = [math.exp(-0.5 * j * j) for j in range(-RADIUS, RADIUS + 1)]
    summed = sum(weights_raw)
    return [value / summed for value in weights_raw]


def band_kernel(flags_ref, joined_ref, band_ref, log_ref, table_ref, smooth, lateral, turned):
    planes, rows, width = log_ref.shape
    taps = gauss_taps()
    zero_rows = jnp.zeros((PAD, width), jnp.float32)

    lateral[0:PAD] = zero_rows
    lateral[PAD + rows :] = zero_rows

    @pl.loop(0, planes + 2)
    def _(z):
        total = taps[RADIUS] * joined_ref[z + RADIUS]
        for j in range(RADIUS):
            total = total + taps[j] * (joined_ref[z + j] + joined_ref[z + 2 * RADIUS - j])
        lateral[PAD : PAD + rows] = total
        down = taps[RADIUS] * total
        for j in range(RADIUS):
            shift = RADIUS - j
            down = down + taps[j] * (
                lateral[PAD - shift : PAD - shift + rows] + lateral[PAD + shift : PAD + shift + rows]
            )
        across = jnp.dot(
            down, band_ref[...], precision=lax.Precision.HIGHEST, preferred_element_type=jnp.float32
        )
        keep = jnp.where(z == 0, flags_ref[0], jnp.where(z == planes + 1, flags_ref[1], 1.0))
        smooth[z, 0:PAD] = zero_rows
        smooth[z, PAD + rows :] = zero_rows
        smooth[z, PAD : PAD + rows] = across * keep

    column = lax.broadcasted_iota(jnp.int32, (rows, width), 1)

    @pl.loop(0, planes)
    def _(z):
        center = smooth[z + 1, PAD : PAD + rows]
        beside = smooth[z, PAD : PAD + rows] + smooth[z + 2, PAD : PAD + rows]
        beside = beside + smooth[z + 1, PAD + 1 : PAD + 1 + rows] + smooth[z + 1, PAD - 1 : PAD - 1 + rows]
        right = jnp.where(column == width - 1, 0.0, pltpu.roll(center, width - 1, 1))
        left = jnp.where(column == 0, 0.0, pltpu.roll(center, 1, 1))
        log_ref[z] = beside + right + left - 6.0 * center

    pitch = turned.shape[0] // (planes // 4 * (rows // 8))

    @pl.loop(0, planes // 4)
    def _(a):
        for b in range(rows // 8):
            parts = [smooth[4 * a + dz + 1, PAD + 8 * b : PAD + 8 * b + 8] for dz in range(4)]
            parts = parts + [log_ref[4 * a + dz, 8 * b : 8 * b + 8] for dz in range(4)]
            block = jnp.concatenate(parts, axis=0)
            block = jnp.concatenate([block, pltpu.roll(block, width - 1, 1)], axis=0)
            start = pl.multiple_of((a * (rows // 8) + b) * pitch, 8)
            turned[pl.ds(start, width)] = block.T

    spots = planes // 4 * (rows // 8)

    @pl.loop(0, width // 8)
    def _(xb):
        for u in range(8):
            x = xb * 8 + u
            table_ref[x] = turned[pl.ds(x, spots, stride=pitch), :].astype(jnp.bfloat16)


def gather_kernel(own_w, own_s, w_ref, s_ref, sems, local):
    tile, slab = lax.axis_index("tile"), lax.axis_index("slab")
    depth = lax.axis_size("tile") // 2
    z, y, x, core = tile // 2, tile % 2, slab // 2, slab % 2
    above, below = (tile + 2, slab), (tile - 2, slab)
    beside, across, twin = (2 * z + 1 - y, slab), (tile, 2 * (1 - x) + core), (tile, 2 * x + 1 - core)
    local_w = pltpu.make_async_copy(own_w, w_ref.at[tile], local.at[0])
    local_s = pltpu.make_async_copy(own_s, s_ref.at[tile], local.at[1])
    local_w.start()
    local_s.start()
    barrier = pltpu.get_barrier_semaphore()

    def greet(peer):
        pl.semaphore_signal(barrier, inc=1, device_id=peer, device_id_type=pl.DeviceIdType.MESH)

    for peer in (beside, across, twin):
        greet(peer)
    pl.when(z < depth - 1)(lambda: greet(above))
    pl.when(z > 0)(lambda: greet(below))
    ends = jnp.where(z == 0, 1, 0) + jnp.where(z == depth - 1, 1, 0)
    pl.semaphore_wait(barrier, 5 - ends)
    local_s.wait()
    local_w.wait()

    def plane_part(origin):
        return w_ref.at[origin, pl.ds(core * 3 + x, 2)]

    def copy(ref, origin, out, into, peer):
        return pltpu.make_async_remote_copy(
            src_ref=ref, dst_ref=ref, send_sem=sems.at[out, origin], recv_sem=sems.at[into, origin],
            device_id=peer, device_id_type=pl.DeviceIdType.MESH,
        )

    sent = []

    def send(cond, *args):
        pl.when(cond)(lambda: copy(*args).start())
        sent.append((cond, args))

    def arrive(cond, ref, origin, into):
        pl.when(cond)(lambda: copy(ref, origin, 0, into, twin).wait_recv())

    always = z >= 0
    not_top, not_bottom = z < depth - 1, z > 0

    def along(cond, origin, upward, downward):
        if upward:
            send(cond & not_top, s_ref.at[origin], origin, 0, 9, above)
        if downward:
            send(cond & not_bottom, s_ref.at[origin], origin, 1, 9, below)
        send(cond, s_ref.at[origin], origin, 2, 9, beside)
        if upward:
            send(cond & not_top, plane_part(origin), origin, 3, 10, above)
        if downward:
            send(cond & not_bottom, plane_part(origin), origin, 4, 10, below)
        send(cond, plane_part(origin), origin, 5, 10, beside)

    def aside(cond, origin):
        send(cond, w_ref.at[origin, core * 3 + 2 * x], origin, 6, 11, across)
        send(cond, plane_part(origin), origin, 7, 12, twin)

    others = []
    along(always, tile, True, True)
    for d in range(depth):
        sides = [(always, z)] if d == 0 else [(z >= d, z - d), (z + d < depth, z + d)]
        for k, (cond, zz) in enumerate(sides):
            if d > 0:
                origin = 2 * zz + y
                arrive(cond, s_ref.at[origin], origin, 9)
                arrive(cond, plane_part(origin), origin, 10)
                along(cond, origin, k == 0, k == 1)
                aside(cond, origin)
                others.append((cond, origin))
        for cond, zz in sides:
            origin = 2 * zz + 1 - y
            arrive(cond, s_ref.at[origin], origin, 9)
            arrive(cond, plane_part(origin), origin, 10)
            aside(cond, origin)
            others.append((cond, origin))
    for cond, origin in others:
        part = w_ref.at[origin, core * 3 + 2 * (1 - x)]
        arrive(cond, part, origin, 11)
        send(cond, part, origin, 8, 13, twin)
    for cond, origin in others:
        arrive(cond, w_ref.at[origin, pl.ds((1 - core) * 3 + x, 2)], origin, 12)
        arrive(cond, w_ref.at[origin, (1 - core) * 3 + 2 * (1 - x)], origin, 13)
    for cond, args in sent:
        pl.when(cond)(lambda args=args: copy(*args).wait_send())


def classify_kernel(starts_ref, routes_ref, table_ref, weights_ref, out_ref):
    def rows_of(route, first, length):
        return weights_ref[route, first : first + length]

    @pl.loop(0, out_ref.shape[0])
    def _(i):
        start = starts_ref[i]
        route = routes_ref[i]
        patches = jnp.concatenate(
            [
                jnp.concatenate([table_ref[start + 8 * c + 2 * j] for j in range(4)], axis=1)
                for c in range(8)
            ],
            axis=0,
        )
        stem = rows_of(route, 0, 512)
        hidden = jnp.dot(patches, stem, preferred_element_type=jnp.float32).astype(jnp.bfloat16)
        wide = hidden.astype(jnp.float32)
        scale = lax.rsqrt(jnp.mean(wide * wide, axis=1, keepdims=True) + 1e-05)
        normed = (wide * scale).astype(jnp.bfloat16)
        expanded = []
        for block in range(4):
            expand = rows_of(route, 512 + block * 256, 256)
            wider = jnp.dot(normed, expand, preferred_element_type=jnp.float32)
            expanded.append(jnp.maximum(wider, 0.0).astype(jnp.bfloat16))
        shrink = rows_of(route, 1536, 1024)
        added = jnp.dot(jnp.concatenate(expanded, axis=1), shrink, preferred_element_type=jnp.float32)
        last = (wide + added).astype(jnp.bfloat16).astype(jnp.float32)
        head = rows_of(route, 2560, 16).astype(jnp.float32)
        total = head[0:8] * jnp.sum(last, axis=0, keepdims=True)
        score = jnp.sum(total, axis=1, keepdims=True) * (1.0 / patches.shape[0])
        out_ref[i] = jnp.broadcast_to(score, out_ref.shape[1:])


def own_weights(stem_weight, expand_weight, shrink_weight, head_weight):
    stem = stem_weight[0].reshape(64, 8, 256).transpose(1, 0, 2).reshape(512, 256)
    expand = [expand_weight[0, 0][:, 256 * m : 256 * m + 256] for m in range(4)]
    head = jnp.pad(head_weight[0].T, ((0, 24), (0, 0)))
    return jnp.concatenate([stem] + expand + [shrink_weight[0, 0], head], axis=0)


def body(
    volume,
    partner,
    offsets,
    starts,
    classifier,
    stem_weight,
    expand_weight,
    shrink_weight,
    head_weight,
):
    slabs, slab_me = lax.axis_size("slab"), lax.axis_index("slab")
    tiles, tile_me = lax.axis_size("tile"), lax.axis_index("tile")
    planes, rows, width = volume.shape[1:]
    raw = volume[0]

    up = [(i, i + 1) for i in range(slabs - 1)]
    down = [(i + 1, i) for i in range(slabs - 1)]
    before = lax.ppermute(raw[planes - HALO :], "slab", up)
    after = lax.ppermute(raw[:HALO], "slab", down)
    raw = jnp.concatenate([before, raw, after], axis=0)
    deep = planes + 2 * HALO
    strip = raw[:, :, :OV].reshape(deep, rows * OV // 128, 128)
    share = own_weights(stem_weight, expand_weight, shrink_weight, head_weight)
    if tiles == 8 and slabs == 4:
        share = share.reshape(6, share.shape[0] // 6, 256)
        anywhere = pl.BlockSpec(memory_space=pl.ANY)
        weights, strips = pl.pallas_call(
            gather_kernel,
            out_shape=(
                jax.ShapeDtypeStruct((tiles,) + share.shape, share.dtype),
                jax.ShapeDtypeStruct((tiles,) + strip.shape, strip.dtype),
            ),
            in_specs=[anywhere, anywhere],
            out_specs=(anywhere, anywhere),
            scratch_shapes=[pltpu.SemaphoreType.DMA((14, tiles)), pltpu.SemaphoreType.DMA((2,))],
            compiler_params=pltpu.CompilerParams(collective_id=0, has_side_effects=True),
            name="gather",
        )(share, strip)
    else:
        strips = lax.all_gather(strip, "tile", axis=0)
        part = share.shape[0] // slabs
        share = lax.dynamic_slice_in_dim(share, slab_me * part, part, axis=0)
        weights = lax.all_gather(share, ("tile", "slab"), axis=0)
    weights = weights.reshape(tiles, -1, 256)

    mate = lax.dynamic_index_in_dim(strips, partner[tile_me], 0, keepdims=False)
    mate = mate.reshape(deep, rows, OV)
    mate = lax.dynamic_slice_in_dim(
        jnp.concatenate([mate, mate], axis=1), rows - offsets[tile_me], rows, axis=1
    ).astype(jnp.float32)
    ramp = 0.25 + 0.5 * (jnp.arange(OV, dtype=jnp.float32) + 0.5) / OV
    values = raw.astype(jnp.float32)
    joined = jnp.concatenate(
        [ramp * values[..., :OV] + (1.0 - ramp) * mate, values[..., OV:]], axis=2
    )

    taps = gauss_taps()
    apart = jnp.arange(width)[:, None] - jnp.arange(width)[None, :]
    band = sum(jnp.where(apart == j - RADIUS, taps[j], 0.0) for j in range(2 * RADIUS + 1))
    flags = jnp.stack([slab_me > 0, slab_me < slabs - 1]).astype(jnp.float32)
    spots = planes // 4 * (rows // 8)
    vmem = pl.BlockSpec(memory_space=pltpu.VMEM)
    smem = pl.BlockSpec(memory_space=pltpu.SMEM)
    log_response, table = pl.pallas_call(
        band_kernel,
        out_shape=(
            jax.ShapeDtypeStruct((planes, rows, width), jnp.float32),
            jax.ShapeDtypeStruct((width, spots, 128), jnp.bfloat16),
        ),
        in_specs=[smem, vmem, vmem],
        out_specs=(vmem, vmem),
        scratch_shapes=[
            pltpu.VMEM((planes + 2, rows + 2 * PAD, width), jnp.float32),
            pltpu.VMEM((rows + 2 * PAD, width), jnp.float32),
            pltpu.VMEM((spots * (width + 8), 128), jnp.float32),
        ],
        compiler_params=pltpu.CompilerParams(vmem_limit_bytes=48 * 1024 * 1024),
        cost_estimate=pl.CostEstimate(flops=10**9, bytes_accessed=6 * 10**6, transcendentals=0),
        name="band",
    )(flags, joined, band)

    count = starts.shape[0]
    scores = pl.pallas_call(
        classify_kernel,
        out_shape=jax.ShapeDtypeStruct((count, 8, 128), jnp.float32),
        in_specs=[smem, smem, vmem, vmem],
        out_specs=vmem,
        compiler_params=pltpu.CompilerParams(vmem_limit_bytes=48 * 1024 * 1024),
        cost_estimate=pl.CostEstimate(flops=54 * 10**8, bytes_accessed=13 * 10**6, transcendentals=0),
        name="classify",
    )(starts, classifier[:, 0], table, weights)
    return log_response[None], scores[:, :, 0]


def solution(mesh):
    return jax.shard_map(
        body,
        mesh=mesh,
        in_specs=(
            P("tile", "slab", None, None),
            P(),
            P(),
            P(("tile", "slab")),
            P(("tile", "slab"), None),
            P("tile", None, None),
            P("tile", None, None, None),
            P("tile", None, None, None),
            P("tile", None, None),
        ),
        out_specs=(P("tile", "slab", None, None), P(("tile", "slab"), None)),
        check_vma=False,
    )
```

```python
import functools
import math

import jax
import jax.numpy as jnp
from jax import lax
from jax.experimental import pallas as pl
from jax.experimental.pallas import tpu as pltpu
from jax.sharding import PartitionSpec as P

OV = 32
RADIUS = 3
HALO = RADIUS + 1
PAD = 8


def gauss_taps():
    weights_raw = [math.exp(-0.5 * j * j) for j in range(-RADIUS, RADIUS + 1)]
    summed = sum(weights_raw)
    return [value / summed for value in weights_raw]


def band_kernel(flags_ref, joined_ref, band_ref, log_ref, table_ref, smooth, lateral, turned):
    planes, rows, width = log_ref.shape
    taps = gauss_taps()
    zero_rows = jnp.zeros((PAD, width), jnp.float32)

    lateral[0:PAD] = zero_rows
    lateral[PAD + rows :] = zero_rows

    @pl.loop(0, planes + 2)
    def _(z):
        total = taps[RADIUS] * joined_ref[z + RADIUS]
        for j in range(RADIUS):
            total = total + taps[j] * (joined_ref[z + j] + joined_ref[z + 2 * RADIUS - j])
        lateral[PAD : PAD + rows] = total
        down = taps[RADIUS] * total
        for j in range(RADIUS):
            shift = RADIUS - j
            down = down + taps[j] * (
                lateral[PAD - shift : PAD - shift + rows] + lateral[PAD + shift : PAD + shift + rows]
            )
        across = jnp.dot(
            down, band_ref[...], precision=lax.Precision.HIGHEST, preferred_element_type=jnp.float32
        )
        keep = jnp.where(z == 0, flags_ref[0], jnp.where(z == planes + 1, flags_ref[1], 1.0))
        smooth[z, 0:PAD] = zero_rows
        smooth[z, PAD + rows :] = zero_rows
        smooth[z, PAD : PAD + rows] = across * keep

    column = lax.broadcasted_iota(jnp.int32, (rows, width), 1)

    @pl.loop(0, planes)
    def _(z):
        center = smooth[z + 1, PAD : PAD + rows]
        beside = smooth[z, PAD : PAD + rows] + smooth[z + 2, PAD : PAD + rows]
        beside = beside + smooth[z + 1, PAD + 1 : PAD + 1 + rows] + smooth[z + 1, PAD - 1 : PAD - 1 + rows]
        right = jnp.where(column == width - 1, 0.0, pltpu.roll(center, width - 1, 1))
        left = jnp.where(column == 0, 0.0, pltpu.roll(center, 1, 1))
        log_ref[z] = beside + right + left - 6.0 * center

    pitch = turned.shape[0] // (planes // 4 * (rows // 8))

    @pl.loop(0, planes // 4)
    def _(a):
        for b in range(rows // 8):
            parts = [smooth[4 * a + dz + 1, PAD + 8 * b : PAD + 8 * b + 8] for dz in range(4)]
            parts = parts + [log_ref[4 * a + dz, 8 * b : 8 * b + 8] for dz in range(4)]
            block = jnp.concatenate(parts, axis=0)
            block = jnp.concatenate([block, pltpu.roll(block, width - 1, 1)], axis=0)
            start = pl.multiple_of((a * (rows // 8) + b) * pitch, 8)
            turned[pl.ds(start, width)] = block.T

    spots = planes // 4 * (rows // 8)

    @pl.loop(0, width // 8)
    def _(xb):
        for u in range(8):
            x = xb * 8 + u
            table_ref[x] = turned[pl.ds(x, spots, stride=pitch), :].astype(jnp.bfloat16)


def strip_kernel(own_ref, strips_ref, sems, local):
    tile, slab = lax.axis_index("tile"), lax.axis_index("slab")
    depth = lax.axis_size("tile") // 2
    z, y = tile // 2, tile % 2
    above, below, beside = (tile + 2, slab), (tile - 2, slab), (2 * z + 1 - y, slab)
    not_top, not_bottom = z < depth - 1, z > 0
    own = pltpu.make_async_copy(own_ref, strips_ref.at[tile], local)
    own.start()
    barrier = pltpu.get_barrier_semaphore()

    def greet(peer):
        pl.semaphore_signal(barrier, inc=1, device_id=peer, device_id_type=pl.DeviceIdType.MESH)

    greet(beside)
    pl.when(not_top)(lambda: greet(above))
    pl.when(not_bottom)(lambda: greet(below))
    ends = jnp.where(z == 0, 1, 0) + jnp.where(z == depth - 1, 1, 0)
    pl.semaphore_wait(barrier, 3 - ends)
    own.wait()
    sent = []

    def copy(origin, out, peer):
        return pltpu.make_async_remote_copy(
            src_ref=strips_ref.at[origin], dst_ref=strips_ref.at[origin],
            send_sem=sems.at[out, origin], recv_sem=sems.at[3, origin],
            device_id=peer, device_id_type=pl.DeviceIdType.MESH,
        )

    def send(cond, *args):
        pl.when(cond)(lambda: copy(*args).start())
        sent.append((cond, args))

    def arrive(cond, origin):
        pl.when(cond)(lambda: copy(origin, 0, beside).wait_recv())

    send(not_top, tile, 0, above)
    send(not_bottom, tile, 1, below)
    send(z >= 0, tile, 2, beside)
    for d in range(1, depth):
        for cond, origin, more, out, onward in (
            (z >= d, tile - 2 * d, not_top, 0, above),
            (z + d < depth, tile + 2 * d, not_bottom, 1, below),
        ):
            arrive(cond, origin)
            send(cond & more, origin, out, onward)
            send(cond, origin, 2, beside)
    arrive(z >= 0, 2 * z + 1 - y)
    for d in range(1, depth):
        arrive(z >= d, 2 * (z - d) + 1 - y)
        arrive(z + d < depth, 2 * (z + d) + 1 - y)
    for cond, args in sent:
        pl.when(cond)(lambda args=args: copy(*args).wait_send())


def classify_kernel(starts_ref, routes_ref, table_ref, weights_ref, out_ref):
    slabs = weights_ref.shape[1]
    stem_rows, expand_rows, shrink_rows = 512 // slabs, 256 // slabs, 1024 // slabs

    def rows_of(route, first, length):
        return jnp.concatenate([weights_ref[route, s, first : first + length] for s in range(slabs)], axis=0)

    @pl.loop(0, out_ref.shape[0], unroll=2)
    def _(i):
        start = starts_ref[i]
        route = routes_ref[i]
        patches = jnp.concatenate(
            [
                jnp.concatenate([table_ref[start + 8 * c + 2 * j] for j in range(4)], axis=1)
                for c in range(8)
            ],
            axis=0,
        )
        stem = rows_of(route, 0, stem_rows)
        hidden = jnp.dot(patches, stem, preferred_element_type=jnp.float32).astype(jnp.bfloat16)
        wide = hidden.astype(jnp.float32)
        scale = lax.rsqrt(jnp.mean(wide * wide, axis=1, keepdims=True) + 1e-05)
        normed = (wide * scale).astype(jnp.bfloat16)
        expanded = []
        for block in range(4):
            expand = rows_of(route, stem_rows + block * expand_rows, expand_rows)
            wider = jnp.dot(normed, expand, preferred_element_type=jnp.float32)
            expanded.append(jnp.maximum(wider, 0.0).astype(jnp.bfloat16))
        shrink = rows_of(route, stem_rows + 4 * expand_rows, shrink_rows)
        added = jnp.dot(jnp.concatenate(expanded, axis=1), shrink, preferred_element_type=jnp.float32)
        last = (wide + added).astype(jnp.bfloat16).astype(jnp.float32)
        head = weights_ref[route, 0, stem_rows + 4 * expand_rows + shrink_rows :].astype(jnp.float32)
        total = head[0:8] * jnp.sum(last, axis=0, keepdims=True)
        score = jnp.sum(total, axis=1, keepdims=True) * (1.0 / patches.shape[0])
        out_ref[i] = jnp.broadcast_to(score, out_ref.shape[1:])


def own_weights(stem_weight, expand_weight, shrink_weight, head_weight):
    slabs, slab_me = lax.axis_size("slab"), lax.axis_index("slab")
    stem, expand, shrink, head = stem_weight[0], expand_weight[0, 0], shrink_weight[0, 0], head_weight[0]
    stem = lax.dynamic_slice_in_dim(stem.reshape(64, 8, 256), slab_me * (8 // slabs), 8 // slabs, axis=1)
    stem = stem.transpose(1, 0, 2).reshape(512 // slabs, 256)
    expand = lax.dynamic_slice_in_dim(expand, slab_me * (256 // slabs), 256 // slabs, axis=0)
    expand = [expand[:, 256 * m : 256 * m + 256] for m in range(4)]
    shrink = lax.dynamic_slice_in_dim(shrink, slab_me * (1024 // slabs), 1024 // slabs, axis=0)
    head = jnp.pad(head.T, ((0, 8), (0, 0)))
    return jnp.concatenate([stem] + expand + [shrink, head], axis=0)


def body(
    volume,
    partner,
    offsets,
    starts,
    classifier,
    stem_weight,
    expand_weight,
    shrink_weight,
    head_weight,
):
    slabs, slab_me = lax.axis_size("slab"), lax.axis_index("slab")
    tiles, tile_me = lax.axis_size("tile"), lax.axis_index("tile")
    planes, rows, width = volume.shape[1:]
    raw = volume[0]

    up = [(i, i + 1) for i in range(slabs - 1)]
    down = [(i + 1, i) for i in range(slabs - 1)]
    before = lax.ppermute(raw[planes - HALO :], "slab", up)
    after = lax.ppermute(raw[:HALO], "slab", down)
    raw = jnp.concatenate([before, raw, after], axis=0)
    deep = planes + 2 * HALO
    strip = raw[:, :, :OV].reshape(deep, rows * OV // 128, 128)
    if tiles == 8 and slabs == 4:
        anywhere = pl.BlockSpec(memory_space=pl.ANY)
        strips = pl.pallas_call(
            strip_kernel,
            out_shape=jax.ShapeDtypeStruct((tiles,) + strip.shape, strip.dtype),
            in_specs=[anywhere],
            out_specs=anywhere,
            scratch_shapes=[pltpu.SemaphoreType.DMA((4, tiles)), pltpu.SemaphoreType.DMA],
            compiler_params=pltpu.CompilerParams(collective_id=0, has_side_effects=True),
            cost_estimate=pl.CostEstimate(flops=0, bytes_accessed=40 * 10**6, transcendentals=0),
            name="strips",
        )(strip)
    else:
        strips = lax.all_gather(strip, "tile", axis=0)

    share = own_weights(stem_weight, expand_weight, shrink_weight, head_weight)
    weights = lax.all_gather(share, ("tile", "slab"), axis=0)
    weights = weights.reshape(tiles, slabs, share.shape[0], 256)

    mate = lax.dynamic_index_in_dim(strips, partner[tile_me], 0, keepdims=False)
    mate = mate.reshape(deep, rows, OV)
    mate = lax.dynamic_slice_in_dim(
        jnp.concatenate([mate, mate], axis=1), rows - offsets[tile_me], rows, axis=1
    ).astype(jnp.float32)
    ramp = 0.25 + 0.5 * (jnp.arange(OV, dtype=jnp.float32) + 0.5) / OV
    values = raw.astype(jnp.float32)
    joined = jnp.concatenate(
        [ramp * values[..., :OV] + (1.0 - ramp) * mate, values[..., OV:]], axis=2
    )

    taps = gauss_taps()
    apart = jnp.arange(width)[:, None] - jnp.arange(width)[None, :]
    band = sum(jnp.where(apart == j - RADIUS, taps[j], 0.0) for j in range(2 * RADIUS + 1))
    flags = jnp.stack([slab_me > 0, slab_me < slabs - 1]).astype(jnp.float32)
    spots = planes // 4 * (rows // 8)
    vmem = pl.BlockSpec(memory_space=pltpu.VMEM)
    smem = pl.BlockSpec(memory_space=pltpu.SMEM)
    log_response, table = pl.pallas_call(
        band_kernel,
        out_shape=(
            jax.ShapeDtypeStruct((planes, rows, width), jnp.float32),
            jax.ShapeDtypeStruct((width, spots, 128), jnp.bfloat16),
        ),
        in_specs=[smem, vmem, vmem],
        out_specs=(vmem, vmem),
        scratch_shapes=[
            pltpu.VMEM((planes + 2, rows + 2 * PAD, width), jnp.float32),
            pltpu.VMEM((rows + 2 * PAD, width), jnp.float32),
            pltpu.VMEM((spots * (width + 8), 128), jnp.float32),
        ],
        compiler_params=pltpu.CompilerParams(vmem_limit_bytes=48 * 1024 * 1024),
        cost_estimate=pl.CostEstimate(flops=10**9, bytes_accessed=6 * 10**6, transcendentals=0),
        name="band",
    )(flags, joined, band)

    count = starts.shape[0]
    scores = pl.pallas_call(
        classify_kernel,
        out_shape=jax.ShapeDtypeStruct((count, 8, 128), jnp.float32),
        in_specs=[smem, smem, vmem, vmem],
        out_specs=vmem,
        compiler_params=pltpu.CompilerParams(vmem_limit_bytes=48 * 1024 * 1024),
        cost_estimate=pl.CostEstimate(flops=54 * 10**8, bytes_accessed=13 * 10**6, transcendentals=0),
        name="classify",
    )(starts, classifier[:, 0], table, weights)
    return log_response[None], scores[:, :, 0]


def solution(mesh):
    return jax.shard_map(
        body,
        mesh=mesh,
        in_specs=(
            P("tile", "slab", None, None),
            P(),
            P(),
            P(("tile", "slab")),
            P(("tile", "slab"), None),
            P("tile", None, None),
            P("tile", None, None, None),
            P("tile", None, None, None),
            P("tile", None, None),
        ),
        out_specs=(P("tile", "slab", None, None), P(("tile", "slab"), None)),
        check_vma=False,
    )
```

```python
import functools
import math

import jax
import jax.numpy as jnp
from jax import lax
from jax.experimental import pallas as pl
from jax.experimental.pallas import tpu as pltpu
from jax.sharding import PartitionSpec as P

OV = 32
CX = 64
RADIUS = 3
HALO = RADIUS + 1
PAD = 8


def gauss_taps():
    weights_raw = [math.exp(-0.5 * j * j) for j in range(-RADIUS, RADIUS + 1)]
    summed = sum(weights_raw)
    return [value / summed for value in weights_raw]


def band_kernel(flags_ref, joined_ref, band_ref, log_ref, table_ref, smooth, lateral, turned):
    planes, rows, width = log_ref.shape
    taps = gauss_taps()
    zero_rows = jnp.zeros((PAD, width), jnp.float32)

    lateral[0:PAD] = zero_rows
    lateral[PAD + rows :] = zero_rows

    @pl.loop(0, planes + 2)
    def _(z):
        total = taps[RADIUS] * joined_ref[z + RADIUS]
        for j in range(RADIUS):
            total = total + taps[j] * (joined_ref[z + j] + joined_ref[z + 2 * RADIUS - j])
        lateral[PAD : PAD + rows] = total
        down = taps[RADIUS] * total
        for j in range(RADIUS):
            shift = RADIUS - j
            down = down + taps[j] * (
                lateral[PAD - shift : PAD - shift + rows] + lateral[PAD + shift : PAD + shift + rows]
            )
        across = jnp.dot(
            down, band_ref[...], precision=lax.Precision.HIGHEST, preferred_element_type=jnp.float32
        )
        keep = jnp.where(z == 0, flags_ref[0], jnp.where(z == planes + 1, flags_ref[1], 1.0))
        smooth[z, 0:PAD] = zero_rows
        smooth[z, PAD + rows :] = zero_rows
        smooth[z, PAD : PAD + rows] = across * keep

    column = lax.broadcasted_iota(jnp.int32, (rows, width), 1)

    @pl.loop(0, planes)
    def _(z):
        center = smooth[z + 1, PAD : PAD + rows]
        beside = smooth[z, PAD : PAD + rows] + smooth[z + 2, PAD : PAD + rows]
        beside = beside + smooth[z + 1, PAD + 1 : PAD + 1 + rows] + smooth[z + 1, PAD - 1 : PAD - 1 + rows]
        right = jnp.where(column == width - 1, 0.0, pltpu.roll(center, width - 1, 1))
        left = jnp.where(column == 0, 0.0, pltpu.roll(center, 1, 1))
        log_ref[z] = beside + right + left - 6.0 * center

    pitch = turned.shape[0] // (planes // 4 * (rows // 8))

    @pl.loop(0, planes // 4)
    def _(a):
        for b in range(rows // 8):
            parts = [smooth[4 * a + dz + 1, PAD + 8 * b : PAD + 8 * b + 8] for dz in range(4)]
            parts = parts + [log_ref[4 * a + dz, 8 * b : 8 * b + 8] for dz in range(4)]
            block = jnp.concatenate(parts, axis=0)
            block = jnp.concatenate([block, pltpu.roll(block, width - 1, 1)], axis=0)
            start = pl.multiple_of((a * (rows // 8) + b) * pitch, 8)
            turned[pl.ds(start, width)] = block.T

    spots = planes // 4 * (rows // 8)

    @pl.loop(0, width // 8)
    def _(xb):
        for u in range(8):
            x = xb * 8 + u
            table_ref[x] = turned[pl.ds(x, spots, stride=pitch), :].astype(jnp.bfloat16)


def strip_kernel(own_ref, strips_ref, sems, local):
    tile, slab = lax.axis_index("tile"), lax.axis_index("slab")
    depth = lax.axis_size("tile") // 2
    z, y = tile // 2, tile % 2
    above, below, beside = (tile + 2, slab), (tile - 2, slab), (2 * z + 1 - y, slab)
    not_top, not_bottom = z < depth - 1, z > 0
    own = pltpu.make_async_copy(own_ref, strips_ref.at[tile], local)
    own.start()
    barrier = pltpu.get_barrier_semaphore()

    def greet(peer):
        pl.semaphore_signal(barrier, inc=1, device_id=peer, device_id_type=pl.DeviceIdType.MESH)

    greet(beside)
    pl.when(not_top)(lambda: greet(above))
    pl.when(not_bottom)(lambda: greet(below))
    ends = jnp.where(z == 0, 1, 0) + jnp.where(z == depth - 1, 1, 0)
    pl.semaphore_wait(barrier, 3 - ends)
    own.wait()
    sent = []

    def copy(origin, out, peer):
        return pltpu.make_async_remote_copy(
            src_ref=strips_ref.at[origin], dst_ref=strips_ref.at[origin],
            send_sem=sems.at[out, origin], recv_sem=sems.at[3, origin],
            device_id=peer, device_id_type=pl.DeviceIdType.MESH,
        )

    def send(cond, *args):
        pl.when(cond)(lambda: copy(*args).start())
        sent.append((cond, args))

    def arrive(cond, origin):
        pl.when(cond)(lambda: copy(origin, 0, beside).wait_recv())

    send(not_top, tile, 0, above)
    send(not_bottom, tile, 1, below)
    send(z >= 0, tile, 2, beside)
    for d in range(1, depth):
        for cond, origin, more, out, onward in (
            (z >= d, tile - 2 * d, not_top, 0, above),
            (z + d < depth, tile + 2 * d, not_bottom, 1, below),
        ):
            arrive(cond, origin)
            send(cond & more, origin, out, onward)
            send(cond, origin, 2, beside)
    arrive(z >= 0, 2 * z + 1 - y)
    for d in range(1, depth):
        arrive(z >= d, 2 * (z - d) + 1 - y)
        arrive(z + d < depth, 2 * (z + d) + 1 - y)
    for cond, args in sent:
        pl.when(cond)(lambda args=args: copy(*args).wait_send())


def rows_of(ref, route, first, length):
    return jnp.concatenate([ref[route, s, first : first + length] for s in range(ref.shape[1])], axis=0)


def expand_kernel(starts_ref, routes_ref, table_ref, weights_ref, hidden_ref, expanded_ref):
    slabs = weights_ref.shape[1]
    stem_rows, expand_rows = 512 // slabs, 256 // slabs
    start = starts_ref[pl.program_id(0)]
    route = routes_ref[pl.program_id(0)]
    patches = jnp.concatenate(
        [
            jnp.concatenate([table_ref[start + 8 * c + 2 * j] for j in range(4)], axis=1)
            for c in range(8)
        ],
        axis=0,
    )
    stem = rows_of(weights_ref, route, 0, stem_rows)
    hidden = jnp.dot(patches, stem, preferred_element_type=jnp.float32).astype(jnp.bfloat16)
    hidden_ref[0] = hidden
    wide = hidden.astype(jnp.float32)
    scale = lax.rsqrt(jnp.mean(wide * wide, axis=1, keepdims=True) + 1e-05)
    normed = (wide * scale).astype(jnp.bfloat16)
    for block in range(4):
        expand = rows_of(weights_ref, route, stem_rows + block * expand_rows, expand_rows)
        wider = jnp.dot(normed, expand, preferred_element_type=jnp.float32)
        expanded_ref[0, :, 256 * block : 256 * block + 256] = jnp.maximum(wider, 0.0).astype(jnp.bfloat16)


def shrink_kernel(routes_ref, hidden_ref, expanded_ref, weights_ref, out_ref):
    route = routes_ref[pl.program_id(0)]
    shrink_rows = 1024 // weights_ref.shape[1]
    shrink = rows_of(weights_ref, route, 0, shrink_rows)
    added = jnp.dot(expanded_ref[0], shrink, preferred_element_type=jnp.float32)
    last = (hidden_ref[0].astype(jnp.float32) + added).astype(jnp.bfloat16).astype(jnp.float32)
    head = weights_ref[route, 0, shrink_rows:].astype(jnp.float32)
    total = head[0:8] * jnp.sum(last, axis=0, keepdims=True)
    score = jnp.sum(total, axis=1, keepdims=True) * (1.0 / last.shape[0])
    out_ref[0] = jnp.broadcast_to(score, out_ref.shape[1:])


def own_weights(stem_weight, expand_weight, shrink_weight, head_weight):
    slabs, slab_me = lax.axis_size("slab"), lax.axis_index("slab")
    stem, expand, shrink, head = stem_weight[0], expand_weight[0, 0], shrink_weight[0, 0], head_weight[0]
    stem = lax.dynamic_slice_in_dim(stem.reshape(64, 8, 256), slab_me * (8 // slabs), 8 // slabs, axis=1)
    stem = stem.transpose(1, 0, 2).reshape(512 // slabs, 256)
    expand = lax.dynamic_slice_in_dim(expand, slab_me * (256 // slabs), 256 // slabs, axis=0)
    expand = [expand[:, 256 * m : 256 * m + 256] for m in range(4)]
    shrink = lax.dynamic_slice_in_dim(shrink, slab_me * (1024 // slabs), 1024 // slabs, axis=0)
    head = jnp.pad(head.T, ((0, 8), (0, 0)))
    return jnp.concatenate([stem] + expand, axis=0), jnp.concatenate([shrink, head], axis=0)


def body(
    volume,
    partner,
    offsets,
    starts,
    classifier,
    stem_weight,
    expand_weight,
    shrink_weight,
    head_weight,
):
    slabs, slab_me = lax.axis_size("slab"), lax.axis_index("slab")
    tiles, tile_me = lax.axis_size("tile"), lax.axis_index("tile")
    planes, rows, width = volume.shape[1:]
    raw = volume[0]

    up = [(i, i + 1) for i in range(slabs - 1)]
    down = [(i + 1, i) for i in range(slabs - 1)]
    before = lax.ppermute(raw[planes - HALO :], "slab", up)
    after = lax.ppermute(raw[:HALO], "slab", down)
    raw = jnp.concatenate([before, raw, after], axis=0)
    deep = planes + 2 * HALO
    strip = raw[:, :, :OV].reshape(deep, rows * OV // 128, 128)
    if tiles == 8 and slabs == 4:
        anywhere = pl.BlockSpec(memory_space=pl.ANY)
        strips = pl.pallas_call(
            strip_kernel,
            out_shape=jax.ShapeDtypeStruct((tiles,) + strip.shape, strip.dtype),
            in_specs=[anywhere],
            out_specs=anywhere,
            scratch_shapes=[pltpu.SemaphoreType.DMA((4, tiles)), pltpu.SemaphoreType.DMA],
            compiler_params=pltpu.CompilerParams(collective_id=0, has_side_effects=True),
            cost_estimate=pl.CostEstimate(flops=0, bytes_accessed=40 * 10**6, transcendentals=0),
            name="strips",
        )(strip)
    else:
        strips = lax.all_gather(strip, "tile", axis=0)

    shares = own_weights(stem_weight, expand_weight, shrink_weight, head_weight)
    early, late = [
        lax.all_gather(share, ("tile", "slab"), axis=0).reshape((tiles, slabs) + share.shape) for share in shares
    ]

    mate = lax.dynamic_index_in_dim(strips, partner[tile_me], 0, keepdims=False)
    mate = mate.reshape(deep, rows, OV)
    mate = lax.dynamic_slice_in_dim(
        jnp.concatenate([mate, mate], axis=1), rows - offsets[tile_me], rows, axis=1
    ).astype(jnp.float32)
    ramp = 0.25 + 0.5 * (jnp.arange(OV, dtype=jnp.float32) + 0.5) / OV
    values = raw.astype(jnp.float32)
    joined = jnp.concatenate(
        [ramp * values[..., :OV] + (1.0 - ramp) * mate, values[..., OV:]], axis=2
    )

    taps = gauss_taps()
    apart = jnp.arange(width)[:, None] - jnp.arange(width)[None, :]
    band = sum(jnp.where(apart == j - RADIUS, taps[j], 0.0) for j in range(2 * RADIUS + 1))
    flags = jnp.stack([slab_me > 0, slab_me < slabs - 1]).astype(jnp.float32)
    spots = planes // 4 * (rows // 8)
    vmem = pl.BlockSpec(memory_space=pltpu.VMEM)
    smem = pl.BlockSpec(memory_space=pltpu.SMEM)
    log_response, table = pl.pallas_call(
        band_kernel,
        out_shape=(
            jax.ShapeDtypeStruct((planes, rows, width), jnp.float32),
            jax.ShapeDtypeStruct((width, spots, 128), jnp.bfloat16),
        ),
        in_specs=[smem, vmem, vmem],
        out_specs=(vmem, vmem),
        scratch_shapes=[
            pltpu.VMEM((planes + 2, rows + 2 * PAD, width), jnp.float32),
            pltpu.VMEM((rows + 2 * PAD, width), jnp.float32),
            pltpu.VMEM((spots * (width + 8), 128), jnp.float32),
        ],
        compiler_params=pltpu.CompilerParams(vmem_limit_bytes=48 * 1024 * 1024),
        cost_estimate=pl.CostEstimate(flops=10**9, bytes_accessed=6 * 10**6, transcendentals=0),
        name="band",
    )(flags, joined, band)

    count = starts.shape[0]
    routes = classifier[:, 0]
    spots_all = rows * planes * CX // 256

    def one(*shape):
        return pl.BlockSpec((1,) + shape, lambda i: (i, 0, 0))

    hidden, expanded = pl.pallas_call(
        expand_kernel,
        grid=(count,),
        out_shape=(
            jax.ShapeDtypeStruct((count, spots_all, 256), jnp.bfloat16),
            jax.ShapeDtypeStruct((count, spots_all, 1024), jnp.bfloat16),
        ),
        in_specs=[smem, smem, vmem, vmem],
        out_specs=(one(spots_all, 256), one(spots_all, 1024)),
        compiler_params=pltpu.CompilerParams(vmem_limit_bytes=48 * 1024 * 1024),
        cost_estimate=pl.CostEstimate(flops=32 * 10**8, bytes_accessed=20 * 10**6, transcendentals=0),
        name="expand",
    )(starts, routes, table, early)
    scores = pl.pallas_call(
        shrink_kernel,
        grid=(count,),
        out_shape=jax.ShapeDtypeStruct((count, 8, 128), jnp.float32),
        in_specs=[smem, one(spots_all, 256), one(spots_all, 1024), vmem],
        out_specs=one(8, 128),
        compiler_params=pltpu.CompilerParams(vmem_limit_bytes=48 * 1024 * 1024),
        cost_estimate=pl.CostEstimate(flops=21 * 10**8, bytes_accessed=15 * 10**6, transcendentals=0),
        name="shrink",
    )(routes, hidden, expanded, late)
    return log_response[None], scores[:, :, 0]


def solution(mesh):
    return jax.shard_map(
        body,
        mesh=mesh,
        in_specs=(
            P("tile", "slab", None, None),
            P(),
            P(),
            P(("tile", "slab")),
            P(("tile", "slab"), None),
            P("tile", None, None),
            P("tile", None, None, None),
            P("tile", None, None, None),
            P("tile", None, None),
        ),
        out_specs=(P("tile", "slab", None, None), P(("tile", "slab"), None)),
        check_vma=False,
    )
```

```python
import functools
import math

import jax
import jax.numpy as jnp
from jax import lax
from jax.experimental import pallas as pl
from jax.experimental.pallas import tpu as pltpu
from jax.sharding import PartitionSpec as P

OV = 32
RADIUS = 3
HALO = RADIUS + 1
PAD = 8


def gauss_taps():
    weights_raw = [math.exp(-0.5 * j * j) for j in range(-RADIUS, RADIUS + 1)]
    summed = sum(weights_raw)
    return [value / summed for value in weights_raw]


def band_kernel(flags_ref, joined_ref, band_ref, log_ref, table_ref, smooth, lateral, turned):
    planes, rows, width = log_ref.shape
    taps = gauss_taps()
    zero_rows = jnp.zeros((PAD, width), jnp.float32)

    lateral[0:PAD] = zero_rows
    lateral[PAD + rows :] = zero_rows

    @pl.loop(0, planes + 2)
    def _(z):
        total = taps[RADIUS] * joined_ref[z + RADIUS]
        for j in range(RADIUS):
            total = total + taps[j] * (joined_ref[z + j] + joined_ref[z + 2 * RADIUS - j])
        lateral[PAD : PAD + rows] = total
        down = taps[RADIUS] * total
        for j in range(RADIUS):
            shift = RADIUS - j
            down = down + taps[j] * (
                lateral[PAD - shift : PAD - shift + rows] + lateral[PAD + shift : PAD + shift + rows]
            )
        across = jnp.dot(
            down, band_ref[...], precision=lax.Precision.HIGHEST, preferred_element_type=jnp.float32
        )
        keep = jnp.where(z == 0, flags_ref[0], jnp.where(z == planes + 1, flags_ref[1], 1.0))
        smooth[z, 0:PAD] = zero_rows
        smooth[z, PAD + rows :] = zero_rows
        smooth[z, PAD : PAD + rows] = across * keep

    column = lax.broadcasted_iota(jnp.int32, (rows, width), 1)

    @pl.loop(0, planes)
    def _(z):
        center = smooth[z + 1, PAD : PAD + rows]
        beside = smooth[z, PAD : PAD + rows] + smooth[z + 2, PAD : PAD + rows]
        beside = beside + smooth[z + 1, PAD + 1 : PAD + 1 + rows] + smooth[z + 1, PAD - 1 : PAD - 1 + rows]
        right = jnp.where(column == width - 1, 0.0, pltpu.roll(center, width - 1, 1))
        left = jnp.where(column == 0, 0.0, pltpu.roll(center, 1, 1))
        log_ref[z] = beside + right + left - 6.0 * center

    pitch = turned.shape[0] // (planes // 4 * (rows // 8))

    @pl.loop(0, planes // 4)
    def _(a):
        for b in range(rows // 8):
            parts = [smooth[4 * a + dz + 1, PAD + 8 * b : PAD + 8 * b + 8] for dz in range(4)]
            parts = parts + [log_ref[4 * a + dz, 8 * b : 8 * b + 8] for dz in range(4)]
            block = jnp.concatenate(parts, axis=0)
            block = jnp.concatenate([block, pltpu.roll(block, width - 1, 1)], axis=0)
            start = pl.multiple_of((a * (rows // 8) + b) * pitch, 8)
            turned[pl.ds(start, width)] = block.T

    spots = planes // 4 * (rows // 8)

    @pl.loop(0, width // 8)
    def _(xb):
        for u in range(8):
            x = xb * 8 + u
            table_ref[x] = turned[pl.ds(x, spots, stride=pitch), :].astype(jnp.bfloat16)


def strip_kernel(own_ref, strips_ref, sems, local):
    tile, slab = lax.axis_index("tile"), lax.axis_index("slab")
    depth = lax.axis_size("tile") // 2
    z, y = tile // 2, tile % 2
    above, below, beside = (tile + 2, slab), (tile - 2, slab), (2 * z + 1 - y, slab)
    not_top, not_bottom = z < depth - 1, z > 0
    own = pltpu.make_async_copy(own_ref, strips_ref.at[tile], local)
    own.start()
    barrier = pltpu.get_barrier_semaphore()

    def greet(peer):
        pl.semaphore_signal(barrier, inc=1, device_id=peer, device_id_type=pl.DeviceIdType.MESH)

    greet(beside)
    pl.when(not_top)(lambda: greet(above))
    pl.when(not_bottom)(lambda: greet(below))
    ends = jnp.where(z == 0, 1, 0) + jnp.where(z == depth - 1, 1, 0)
    pl.semaphore_wait(barrier, 3 - ends)
    own.wait()
    sent = []

    def copy(origin, out, peer):
        return pltpu.make_async_remote_copy(
            src_ref=strips_ref.at[origin], dst_ref=strips_ref.at[origin],
            send_sem=sems.at[out, origin], recv_sem=sems.at[3, origin],
            device_id=peer, device_id_type=pl.DeviceIdType.MESH,
        )

    def send(cond, *args):
        pl.when(cond)(lambda: copy(*args).start())
        sent.append((cond, args))

    def arrive(cond, origin):
        pl.when(cond)(lambda: copy(origin, 0, beside).wait_recv())

    send(not_top, tile, 0, above)
    send(not_bottom, tile, 1, below)
    send(z >= 0, tile, 2, beside)
    for d in range(1, depth):
        for cond, origin, more, out, onward in (
            (z >= d, tile - 2 * d, not_top, 0, above),
            (z + d < depth, tile + 2 * d, not_bottom, 1, below),
        ):
            arrive(cond, origin)
            send(cond & more, origin, out, onward)
            send(cond, origin, 2, beside)
    arrive(z >= 0, 2 * z + 1 - y)
    for d in range(1, depth):
        arrive(z >= d, 2 * (z - d) + 1 - y)
        arrive(z + d < depth, 2 * (z + d) + 1 - y)
    for cond, args in sent:
        pl.when(cond)(lambda args=args: copy(*args).wait_send())


def classify_kernel(starts_ref, routes_ref, table_ref, weights_ref, out_ref):
    slabs = weights_ref.shape[1]
    stem_rows, expand_rows, shrink_rows = 512 // slabs, 256 // slabs, 1024 // slabs

    def rows_of(route, first, length):
        return jnp.concatenate([weights_ref[route, s, first : first + length] for s in range(slabs)], axis=0)

    @pl.loop(0, out_ref.shape[0], unroll=4)
    def _(i):
        start = starts_ref[i]
        route = routes_ref[i]
        patches = jnp.concatenate(
            [
                jnp.concatenate([table_ref[start + 8 * c + 2 * j] for j in range(4)], axis=1)
                for c in range(8)
            ],
            axis=0,
        )
        stem = rows_of(route, 0, stem_rows)
        hidden = jnp.dot(patches, stem, preferred_element_type=jnp.float32).astype(jnp.bfloat16)
        wide = hidden.astype(jnp.float32)
        scale = lax.rsqrt(jnp.mean(wide * wide, axis=1, keepdims=True) + 1e-05)
        normed = (wide * scale).astype(jnp.bfloat16)
        expanded = []
        for block in range(4):
            expand = rows_of(route, stem_rows + block * expand_rows, expand_rows)
            wider = jnp.dot(normed, expand, preferred_element_type=jnp.float32)
            expanded.append(jnp.maximum(wider, 0.0).astype(jnp.bfloat16))
        shrink = rows_of(route, stem_rows + 4 * expand_rows, shrink_rows)
        added = jnp.dot(jnp.concatenate(expanded, axis=1), shrink, preferred_element_type=jnp.float32)
        last = (wide + added).astype(jnp.bfloat16).astype(jnp.float32)
        head = weights_ref[route, 0, stem_rows + 4 * expand_rows + shrink_rows :].astype(jnp.float32)
        total = head[0:8] * jnp.sum(last, axis=0, keepdims=True)
        score = jnp.sum(total, axis=1, keepdims=True) * (1.0 / patches.shape[0])
        out_ref[i] = jnp.broadcast_to(score, out_ref.shape[1:])


def own_weights(stem_weight, expand_weight, shrink_weight, head_weight):
    slabs, slab_me = lax.axis_size("slab"), lax.axis_index("slab")
    stem, expand, shrink, head = stem_weight[0], expand_weight[0, 0], shrink_weight[0, 0], head_weight[0]
    stem = lax.dynamic_slice_in_dim(stem.reshape(64, 8, 256), slab_me * (8 // slabs), 8 // slabs, axis=1)
    stem = stem.transpose(1, 0, 2).reshape(512 // slabs, 256)
    expand = lax.dynamic_slice_in_dim(expand, slab_me * (256 // slabs), 256 // slabs, axis=0)
    expand = [expand[:, 256 * m : 256 * m + 256] for m in range(4)]
    shrink = lax.dynamic_slice_in_dim(shrink, slab_me * (1024 // slabs), 1024 // slabs, axis=0)
    head = jnp.pad(head.T, ((0, 8), (0, 0)))
    return jnp.concatenate([stem] + expand + [shrink, head], axis=0)


def body(
    volume,
    partner,
    offsets,
    starts,
    classifier,
    stem_weight,
    expand_weight,
    shrink_weight,
    head_weight,
):
    slabs, slab_me = lax.axis_size("slab"), lax.axis_index("slab")
    tiles, tile_me = lax.axis_size("tile"), lax.axis_index("tile")
    planes, rows, width = volume.shape[1:]
    raw = volume[0]

    up = [(i, i + 1) for i in range(slabs - 1)]
    down = [(i + 1, i) for i in range(slabs - 1)]
    before = lax.ppermute(raw[planes - HALO :], "slab", up)
    after = lax.ppermute(raw[:HALO], "slab", down)
    raw = jnp.concatenate([before, raw, after], axis=0)
    deep = planes + 2 * HALO
    strip = raw[:, :, :OV].reshape(deep, rows * OV // 128, 128)
    if tiles == 8 and slabs == 4:
        anywhere = pl.BlockSpec(memory_space=pl.ANY)
        strips = pl.pallas_call(
            strip_kernel,
            out_shape=jax.ShapeDtypeStruct((tiles,) + strip.shape, strip.dtype),
            in_specs=[anywhere],
            out_specs=anywhere,
            scratch_shapes=[pltpu.SemaphoreType.DMA((4, tiles)), pltpu.SemaphoreType.DMA],
            compiler_params=pltpu.CompilerParams(collective_id=0, has_side_effects=True),
            cost_estimate=pl.CostEstimate(flops=0, bytes_accessed=40 * 10**6, transcendentals=0),
            name="strips",
        )(strip)
    else:
        strips = lax.all_gather(strip, "tile", axis=0)

    share = own_weights(stem_weight, expand_weight, shrink_weight, head_weight)
    weights = lax.all_gather(share, ("tile", "slab"), axis=0)
    weights = weights.reshape(tiles, slabs, share.shape[0], 256)

    mate = lax.dynamic_index_in_dim(strips, partner[tile_me], 0, keepdims=False)
    mate = mate.reshape(deep, rows, OV)
    mate = lax.dynamic_slice_in_dim(
        jnp.concatenate([mate, mate], axis=1), rows - offsets[tile_me], rows, axis=1
    ).astype(jnp.float32)
    ramp = 0.25 + 0.5 * (jnp.arange(OV, dtype=jnp.float32) + 0.5) / OV
    values = raw.astype(jnp.float32)
    joined = jnp.concatenate(
        [ramp * values[..., :OV] + (1.0 - ramp) * mate, values[..., OV:]], axis=2
    )

    taps = gauss_taps()
    apart = jnp.arange(width)[:, None] - jnp.arange(width)[None, :]
    band = sum(jnp.where(apart == j - RADIUS, taps[j], 0.0) for j in range(2 * RADIUS + 1))
    flags = jnp.stack([slab_me > 0, slab_me < slabs - 1]).astype(jnp.float32)
    spots = planes // 4 * (rows // 8)
    vmem = pl.BlockSpec(memory_space=pltpu.VMEM)
    smem = pl.BlockSpec(memory_space=pltpu.SMEM)
    log_response, table = pl.pallas_call(
        band_kernel,
        out_shape=(
            jax.ShapeDtypeStruct((planes, rows, width), jnp.float32),
            jax.ShapeDtypeStruct((width, spots, 128), jnp.bfloat16),
        ),
        in_specs=[smem, vmem, vmem],
        out_specs=(vmem, vmem),
        scratch_shapes=[
            pltpu.VMEM((planes + 2, rows + 2 * PAD, width), jnp.float32),
            pltpu.VMEM((rows + 2 * PAD, width), jnp.float32),
            pltpu.VMEM((spots * (width + 8), 128), jnp.float32),
        ],
        compiler_params=pltpu.CompilerParams(vmem_limit_bytes=48 * 1024 * 1024),
        cost_estimate=pl.CostEstimate(flops=10**9, bytes_accessed=6 * 10**6, transcendentals=0),
        name="band",
    )(flags, joined, band)

    count = starts.shape[0]
    scores = pl.pallas_call(
        classify_kernel,
        out_shape=jax.ShapeDtypeStruct((count, 8, 128), jnp.float32),
        in_specs=[smem, smem, vmem, vmem],
        out_specs=vmem,
        compiler_params=pltpu.CompilerParams(vmem_limit_bytes=48 * 1024 * 1024),
        cost_estimate=pl.CostEstimate(flops=54 * 10**8, bytes_accessed=13 * 10**6, transcendentals=0),
        name="classify",
    )(starts, classifier[:, 0], table, weights)
    return log_response[None], scores[:, :, 0]


def solution(mesh):
    return jax.shard_map(
        body,
        mesh=mesh,
        in_specs=(
            P("tile", "slab", None, None),
            P(),
            P(),
            P(("tile", "slab")),
            P(("tile", "slab"), None),
            P("tile", None, None),
            P("tile", None, None, None),
            P("tile", None, None, None),
            P("tile", None, None),
        ),
        out_specs=(P("tile", "slab", None, None), P(("tile", "slab"), None)),
        check_vma=False,
    )
```
